32 devices in a mesh: lat: 2 (over x), lon: 16 (over z, y, core).
Axes of the slice: x: 2, y: 2, z: 4, core: 2. Of those that a mesh axis runs over, the one named last changes fastest.
Arguments:
- ocean_field: bfloat16 [32, 256, 256], P('lat', 'lon'), may hold values from -6 to 6
- ocean_mask: int32 [32, 256], P('lat', 'lon'), may hold values from 0 to 1, as said below
- kernels: float32 [4, 7, 7, 256], replicated, may hold values from -0.875 to 0.875
- gains: float32 [4, 256], replicated, may hold values from 0.1 to 1.9
- w_in: bfloat16 [4, 256, 1024], replicated, may hold values from -0.375 to 0.375
- b_in: float32 [4, 1024], replicated, may hold values from -6 to 6
- w_out: bfloat16 [4, 1024, 256], replicated, may hold values from -0.1875 to 0.1875
Outputs:
- new_field: bfloat16 [32, 256, 256], P('lat', 'lon')
The draws below stay inside these ranges and needn't reach their ends.
Inputs may be any that keep to these rules, and one draw needn't show every extreme that they name: `ocean_mask`: each device's tile of 16 x 16 cells holds at most 192 wet cells; some tile holds exactly 192, and some tiles hold none.
All inputs are finite; a program needn't handle non-finite values.
Results may differ from the reference program's by a relative error of at most 0.0095.
Values may be sent and summed in bfloat16 or wider, within the bound.
A program may use at most 64 MiB of HBM per device.

```python
import jax
import jax.numpy as jnp
from jax import lax

TY = 16
TX = 16
C = 256
H = 1024
LAYERS = 4
NY = 32
NX = 256
WET_MAX = 192


def draw_ocean_mask(key, part):
    tile_count = NY // TY * (NX // TX)
    cell_count = TY * TX
    key_count = jax.random.fold_in(key, 11)
    key_full = jax.random.fold_in(key, 12)
    key_order = jax.random.fold_in(key, 13)
    key_dry = jax.random.fold_in(key, 14)
    key_pick = jax.random.fold_in(key, 15)
    wet_counts = jax.random.randint(key_count, (tile_count,), cell_count // 4, WET_MAX + 1)
    dry_draw = jax.random.randint(key_dry, (tile_count,), 0, 10) < 3
    wet_counts = jnp.where(dry_draw, 0, wet_counts)
    full_tile = jax.random.randint(key_full, (), 0, tile_count)
    dry_tile = (full_tile + 1 + jax.random.randint(key_pick, (), 0, tile_count - 1)) % tile_count
    tile_ids = jnp.arange(tile_count)
    wet_counts = jnp.where(tile_ids == dry_tile, 0, wet_counts)
    wet_counts = jnp.where(tile_ids == full_tile, WET_MAX, wet_counts)
    tile_keys = jax.random.split(key_order, tile_count)
    rank_order = jax.vmap(lambda one_key: jax.random.permutation(one_key, cell_count))(tile_keys)
    wet_cells = (rank_order < wet_counts[:, None]).astype(jnp.int32)
    wet_cells = wet_cells.reshape(NY // TY, NX // TX, TY, TX).transpose(0, 2, 1, 3)
    return wet_cells.reshape(NY, NX)


def block_scale(own_key, shape, shards, smallest, top_value):
    loudness, own = 1.0, jax.random.fold_in(own_key, 6)
    for position, shards_of in shards:
        heights = jnp.exp(jax.random.uniform(jax.random.fold_in(own, position), (shards_of,), jnp.float32, smallest / len(shards), top_value / len(shards)))
        loudness = loudness * jnp.repeat(heights, shape[position] // shards_of).reshape([-1 if axis == position else 1 for axis in range(len(shape))])
    return loudness


def noise(key, shape, width, limit, cuts=(), kind=jnp.bfloat16):
    drawn = jax.random.normal(key, shape, jnp.float32) * width
    if len(cuts) > 0:
        drawn = block_scale(key, shape, cuts, -0.22, 0.18) * drawn
    return jnp.clip(drawn, min=-limit, max=limit).astype(kind)


def setup_inputs(seed: int = 0) -> dict:
    seeds = jax.random.split(jax.random.key(seed), 8)
    ocean_field = noise(seeds[0], (NY, NX, C), 1.0, 6.0, ((0, 2), (1, 16)))
    ocean_mask = draw_ocean_mask(jax.random.fold_in(seeds[7], 71), 0)
    kernels = noise(seeds[2], (LAYERS, 7, 7, C), 49 ** -0.5, 0.875, (), jnp.float32)
    gains = jnp.clip(1.0 + 0.18 * jax.random.normal(seeds[3], (LAYERS, C), jnp.float32), 0.1, 1.9)
    w_in = noise(seeds[4], (LAYERS, C, H), C ** -0.5, 0.375)
    b_in = noise(seeds[5], (LAYERS, H), 1.0, 6.0, (), jnp.float32)
    w_out = noise(seeds[6], (LAYERS, H, C), H ** -0.5, 0.1875)
    return dict(ocean_field=ocean_field, ocean_mask=ocean_mask, kernels=kernels, gains=gains, w_in=w_in, b_in=b_in, w_out=w_out)


def cos_rows(row_start, row_count, total_rows):
    globe_rows = row_start + jnp.arange(row_count, dtype=jnp.int32)
    latitude = jnp.pi * ((globe_rows.astype(jnp.float32) + 0.5) / total_rows - 0.5)
    inside = (globe_rows >= 0) & (globe_rows < total_rows)
    return jnp.where(inside, jnp.cos(latitude), jnp.float32(0.0))

def metric_conv(padded, kernel, row_cos):
    out_rows = padded.shape[0] - 6
    out_cols = padded.shape[1] - 6
    scaled = padded.astype(jnp.float32) * row_cos[:, None, None]
    summed = jnp.zeros((out_rows, out_cols, padded.shape[2]), jnp.float32)
    for a in range(7):
        for b in range(7):
            summed = summed + kernel[a, b] * scaled[a:a + out_rows, b:b + out_cols]
    row_weight = row_cos[0:out_rows]
    for a in range(1, 7):
        row_weight = row_weight + row_cos[a:a + out_rows]
    return summed * (7.0 / row_weight)[:, None, None]

def dense_mix(state_now, stencil, wet_mask, gain_vec, w_first, b_first, w_second):
    channels = state_now.shape[-1]
    mean_square = lax.optimization_barrier(jnp.mean(stencil * stencil, axis=-1, keepdims=True))
    normed = (stencil * lax.rsqrt(mean_square + 1e-06) * gain_vec).astype(jnp.bfloat16)
    flat_rows = normed.reshape(-1, channels)
    hidden = jax.nn.silu(jnp.dot(flat_rows, w_first, preferred_element_type=jnp.float32) + b_first).astype(jnp.bfloat16)
    update = jnp.dot(hidden, w_second, preferred_element_type=jnp.float32).reshape(stencil.shape)
    return ((state_now.astype(jnp.float32) + update) * wet_mask[..., None].astype(jnp.float32)).astype(jnp.bfloat16)

def reference(ocean_field, ocean_mask, kernels, gains, w_in, b_in, w_out):
    state_now = ocean_field
    row_cos = cos_rows(-3, NY + 6, NY)
    for layer_index in range(kernels.shape[0]):
        padded = jnp.pad(state_now, ((3, 3), (0, 0), (0, 0)))
        padded = jnp.concatenate([padded[:, -3:], padded, padded[:, :3]], axis=1)
        stencil = metric_conv(padded, kernels[layer_index], row_cos)
        blocks = NY // TY

        def one_block(pieces):
            return dense_mix(pieces[0], pieces[1], pieces[2], gains[layer_index], w_in[layer_index], b_in[layer_index], w_out[layer_index])
        mixed = lax.map(one_block, (state_now.reshape(blocks, TY, NX, C), stencil.reshape(blocks, TY, NX, C), ocean_mask.reshape(blocks, TY, NX)))
        state_now = mixed.reshape(NY, NX, C)
    return state_now
```

```python
import functools

import jax
import jax.numpy as jnp
import numpy as np
from jax import lax
from jax.experimental import pallas as pl
from jax.experimental.pallas import tpu as pltpu
from jax.sharding import PartitionSpec as P

MESH = pl.DeviceIdType.MESH
LEFT, RIGHT, UP, UP_LEFT, UP_RIGHT, DOWN, DOWN_LEFT, DOWN_RIGHT = range(8)


def row_tables(lat_count, tile_rows):
    total = lat_count * tile_rows
    rows = np.arange(-3, total + 3)
    cosine = np.cos(np.pi * ((rows + 0.5) / total - 0.5))
    cosine = np.where((rows >= 0) & (rows < total), cosine, 0.0)
    table = np.zeros((lat_count, 48), np.float32)
    for i in range(lat_count):
        near = cosine[i * tile_rows : i * tile_rows + tile_rows + 6]
        weight = sum(near[a : a + tile_rows] for a in range(7))
        table[i, : tile_rows + 6] = near
        table[i, 24 : 24 + tile_rows] = 7.0 / weight
    return table


def pick_matrix(tile):
    pick = np.zeros((2, 3 * tile, tile * tile), np.float32)
    for r in range(tile):
        for j in range(3):
            pick[0, 3 * r + j, r * tile + j] = 1.0
            pick[1, 3 * r + j, r * tile + tile - 3 + j] = 1.0
    return pick.reshape(6 * tile, tile * tile)


def place_matrix(tile):
    rows = tile + 6
    place = np.zeros((2, rows * 8, 3 * tile + 32), np.float32)
    for r in range(rows):
        for j in range(3):
            if r < 3:
                source = 7 + 3 * r + j
            elif r < 3 + tile:
                source = 16 + 3 * (r - 3) + j
            else:
                source = 16 + 3 * tile + 3 * (r - 3 - tile) + j
            place[0, r * 8 + 5 + j, source] = 1.0
            place[1, r * 8 + j, source] = 1.0
    return place


def kernel(
    lat_count, lon_count, layers,
    table_s, x_h, mask_h, taps_h, gains_h, w_in_h, b_in_h, w_out_h, pick_h, place_h,
    out_h,
    state, field, part, mask_i, mask_f, cos_v, inv_v, taps, gains, w_in, b_in, w_out, pick, place,
    send_cols, recv_cols, recv_rows, load_sem, w_sem, send_sem, recv_sem,
):
    lat, lon = lax.axis_index("lat"), lax.axis_index("lon")
    left, right = lax.rem(lon + lon_count - 1, lon_count), lax.rem(lon + 1, lon_count)
    has_up, has_down = lat > 0, lat < lat_count - 1

    small = [
        pltpu.make_async_copy(src, dst, load_sem.at[i])
        for i, (src, dst) in enumerate(
            [
                (x_h, state.at[0]), (pick_h, pick), (mask_h, mask_i), (taps_h, taps),
                (place_h, place), (gains_h, gains), (b_in_h, b_in),
            ]
        )
    ]

    def weights(l):
        return (
            pltpu.make_async_copy(w_in_h.at[l], w_in.at[l], w_sem.at[0, l]),
            pltpu.make_async_copy(w_out_h.at[l], w_out.at[l], w_sem.at[1, l]),
        )

    for copy in small:
        copy.start()
    for l in range(layers):
        for copy in weights(l):
            copy.start()

    barrier = pltpu.get_barrier_semaphore()

    def greet(to_lat, to_lon):
        pl.semaphore_signal(barrier, inc=1, device_id=(to_lat, to_lon), device_id_type=MESH)

    greet(lat, left)
    greet(lat, right)

    @pl.when(has_up)
    def _():
        for other in (left, lon, right):
            greet(lat - 1, other)

    @pl.when(has_down)
    def _():
        for other in (left, lon, right):
            greet(lat + 1, other)

    @pl.when(jnp.logical_not(has_up))
    def _():
        recv_cols[:, :, 0:16] = jnp.zeros((layers, 2, 16, 256), jnp.bfloat16)
        recv_rows[:, 0] = jnp.zeros((layers, 3, 16, 256), jnp.bfloat16)

    @pl.when(jnp.logical_not(has_down))
    def _():
        recv_cols[:, :, 64:80] = jnp.zeros((layers, 2, 16, 256), jnp.bfloat16)
        recv_rows[:, 1] = jnp.zeros((layers, 3, 16, 256), jnp.bfloat16)

    for r in range(22):
        cos_v[r] = jnp.full((16, 128), table_s[lat, r], jnp.float32)
    for r in range(16):
        inv_v[r] = jnp.full((8, 128), table_s[lat, 24 + r], jnp.float32)

    small[2].wait()
    eye = lax.broadcasted_iota(jnp.int32, (16, 16), 0) == lax.broadcasted_iota(jnp.int32, (16, 16), 1)
    for r in range(16):
        cells = jnp.where(eye, mask_i[r : r + 1, :].astype(jnp.float32), 0.0)
        mask_f[r] = jnp.broadcast_to(jnp.sum(cells, axis=1, keepdims=True), (16, 128))
    small[0].wait()
    small[1].wait()

    def store_own(rows, cells, first):
        scale = cos_v[3 + first : 3 + first + rows]
        for half in range(2):
            field[half, 3 + first : 3 + first + rows, 8:24, :] = cells[:, :, half * 128 : half * 128 + 128] * scale

    store_own(16, state[0].astype(jnp.float32), 0)

    lats = 1
    for there in (has_up, has_down):
        lats = lats + there.astype(jnp.int32)
    pl.semaphore_wait(barrier, 3 * lats - 1)

    def copies(l):
        def remote(kind, src, dst, to_lat, to_lon):
            return pltpu.make_async_remote_copy(
                src_ref=src, dst_ref=dst, send_sem=send_sem.at[l, kind], recv_sem=recv_sem.at[l, kind],
                device_id=(to_lat, to_lon), device_id_type=MESH,
            )

        def side(kind, s, to_lon):
            return remote(kind, send_cols.at[l, s], recv_cols.at[l, 1 - s, 16:64], lat, to_lon)

        def corner(kind, s, src, dst, to_lat, to_lon):
            return remote(
                kind, send_cols.at[l, s, src : src + 16], recv_cols.at[l, 1 - s, dst : dst + 16], to_lat, to_lon
            )

        sides = [side(LEFT, 0, left), side(RIGHT, 1, right)]
        ups = [
            remote(UP, state.at[l, 0:3], recv_rows.at[l, 1], lat - 1, lon),
            corner(UP_LEFT, 0, 0, 64, lat - 1, left),
            corner(UP_RIGHT, 1, 0, 64, lat - 1, right),
        ]
        downs = [
            remote(DOWN, state.at[l, 13:16], recv_rows.at[l, 0], lat + 1, lon),
            corner(DOWN_LEFT, 0, 32, 0, lat + 1, left),
            corner(DOWN_RIGHT, 1, 32, 0, lat + 1, right),
        ]
        return sides, ups, downs

    def local_columns(g):
        return range(3, 7) if g == 0 else range(0, 4)

    def far_columns(g):
        return range(0, 3) if g == 0 else range(4, 7)

    def layer(l, carry):
        edges = jnp.dot(pick[...], state[l].reshape(256, 256), preferred_element_type=jnp.float32)
        edges = edges.astype(jnp.bfloat16)
        send_cols[l, 0] = edges[0:48]
        send_cols[l, 1] = edges[48:96]
        sides, ups, downs = copies(l)
        for copy in sides:
            copy.start()

        @pl.when(has_up)
        def _():
            for copy in ups:
                copy.start()

        @pl.when(has_down)
        def _():
            for copy in downs:
                copy.start()

        @pl.when(l == 0)
        def _():
            for copy in small[3:]:
                copy.wait()

        def weight(half, a, b):
            lanes = pl.ds(pl.multiple_of(half * 128, 128), 128)
            return taps[l, a, b : b + 1, lanes]

        def near(half, carry):
            for g in range(2):
                acc = jnp.zeros((16, 8, 128), jnp.float32)
                for b in local_columns(g):
                    start = 5 + 8 * g + b
                    x = field[half, 3:19, start : start + 8, :]
                    for a in range(7):
                        low, high = max(0, 3 - a), min(16, 19 - a)
                        add = acc[low:high] + weight(half, a, b) * x[low + a - 3 : high + a - 3]
                        pieces = [acc[:low]] * (low > 0) + [add] + [acc[high:]] * (high < 16)
                        acc = jnp.concatenate(pieces, axis=0) if len(pieces) > 1 else add
                part[half, :, 8 * g : 8 * g + 8, :] = acc
            return carry

        lax.fori_loop(0, 2, near, 0)

        for copy in sides:
            copy.wait_recv()

        @pl.when(has_down)
        def _():
            for copy in ups:
                copy.wait_recv()

        @pl.when(has_up)
        def _():
            for copy in downs:
                copy.wait_recv()

        for s in range(2):
            cells = recv_rows[l, s].astype(jnp.float32)
            scale = cos_v[19 * s : 19 * s + 3]
            columns = jnp.dot(place[s], recv_cols[l, s], preferred_element_type=jnp.float32).reshape(22, 8, 256)
            for half in range(2):
                lanes = slice(half * 128, half * 128 + 128)
                field[half, 19 * s : 19 * s + 3, 8:24, :] = cells[:, :, lanes] * scale
                field[half, :, 24 * s : 24 * s + 8, :] = columns[:, :, lanes] * cos_v[:, 0:8, :]

        def far(half, carry):
            for g in range(2):
                acc = part[half, :, 8 * g : 8 * g + 8, :]
                for b in far_columns(g):
                    start = 5 + 8 * g + b
                    x = field[half, :, start : start + 8, :]
                    for a in range(7):
                        acc = acc + weight(half, a, b) * x[a : a + 16]
                top, mid, low = acc[0:3], acc[3:13], acc[13:16]
                for b in local_columns(g):
                    start = 5 + 8 * g + b
                    above = field[half, 0:3, start : start + 8, :]
                    below = field[half, 19:22, start : start + 8, :]
                    for a in range(3):
                        add = top[0 : 3 - a] + weight(half, a, b) * above[a:3]
                        top = jnp.concatenate([add, top[3 - a :]], axis=0) if a > 0 else add
                    for a in range(4, 7):
                        add = low[6 - a :] + weight(half, a, b) * below[0 : a - 3]
                        low = jnp.concatenate([low[: 6 - a], add], axis=0) if a < 6 else add
                acc = jnp.concatenate([top, mid, low], axis=0) * inv_v[...]
                part[half, :, 8 * g : 8 * g + 8, :] = acc
            return carry

        lax.fori_loop(0, 2, far, 0)

        for copy in weights(l):
            copy.wait()
        gain = gains[pl.ds(l, 1), :]
        bias = b_in[pl.ds(l, 1), :]
        rows = 8
        for block in range(2):
            first = block * rows
            s0 = part[0, first : first + rows].reshape(rows * 16, 128)
            s1 = part[1, first : first + rows].reshape(rows * 16, 128)
            mean = jnp.sum(s0 * s0 + s1 * s1, axis=1, keepdims=True) * (1.0 / 256.0)
            scale = lax.rsqrt(mean + 1e-06)
            normed = jnp.concatenate([s0 * scale * gain[:, :128], s1 * scale * gain[:, 128:]], axis=1)
            half_v = 0.5 * (
                jnp.dot(normed.astype(jnp.bfloat16), w_in[l], preferred_element_type=jnp.float32) + bias
            )
            hidden = (half_v + half_v * jnp.tanh(half_v)).astype(jnp.bfloat16)
            update = jnp.dot(hidden, w_out[l], preferred_element_type=jnp.float32).reshape(rows, 16, 256)
            old = state[l, first : first + rows].astype(jnp.float32)
            wet = mask_f[first : first + rows]
            new = ((old + update) * jnp.concatenate([wet, wet], axis=2)).astype(jnp.bfloat16)
            state[l + 1, first : first + rows] = new
            store_own(rows, new.astype(jnp.float32), first)
        return carry

    lax.fori_loop(0, layers, layer, 0)

    final = pltpu.make_async_copy(state.at[layers], out_h, load_sem.at[7])
    final.start()

    def drain(l, carry):
        sides, ups, downs = copies(l)
        for copy in sides:
            copy.wait_send()

        @pl.when(has_up)
        def _():
            for copy in ups:
                copy.wait_send()

        @pl.when(has_down)
        def _():
            for copy in downs:
                copy.wait_send()

        return carry

    lax.fori_loop(0, layers, drain, 0)
    final.wait()


def local(lat_count, lon_count, ocean_field, ocean_mask, kernels, gains, w_in, b_in, w_out):
    layers = kernels.shape[0]
    bf16, f32 = jnp.bfloat16, jnp.float32
    table = jnp.asarray(row_tables(lat_count, ocean_field.shape[0]))
    pick = jnp.asarray(pick_matrix(16), bf16)
    place = jnp.asarray(place_matrix(16), bf16)
    anywhere = pl.BlockSpec(memory_space=pl.ANY)
    return pl.pallas_call(
        functools.partial(kernel, lat_count, lon_count, layers),
        out_shape=jax.ShapeDtypeStruct(ocean_field.shape, bf16),
        in_specs=[pl.BlockSpec(memory_space=pltpu.SMEM)] + [anywhere] * 9,
        out_specs=anywhere,
        scratch_shapes=[
            pltpu.VMEM((layers + 1, 16, 16, 256), bf16),
            pltpu.VMEM((2, 22, 32, 128), f32),
            pltpu.VMEM((2, 16, 16, 128), f32),
            pltpu.VMEM((16, 16), jnp.int32),
            pltpu.VMEM((16, 16, 128), f32),
            pltpu.VMEM((22, 16, 128), f32),
            pltpu.VMEM((16, 8, 128), f32),
            pltpu.VMEM(kernels.shape, f32),
            pltpu.VMEM(gains.shape, f32),
            pltpu.VMEM(w_in.shape, bf16),
            pltpu.VMEM(b_in.shape, f32),
            pltpu.VMEM(w_out.shape, bf16),
            pltpu.VMEM(pick.shape, bf16),
            pltpu.VMEM(place.shape, bf16),
            pltpu.VMEM((layers, 2, 48, 256), bf16),
            pltpu.VMEM((layers, 2, 80, 256), bf16),
            pltpu.VMEM((layers, 2, 3, 16, 256), bf16),
            pltpu.SemaphoreType.DMA((8,)),
            pltpu.SemaphoreType.DMA((2, layers)),
            pltpu.SemaphoreType.DMA((layers, 8)),
            pltpu.SemaphoreType.DMA((layers, 8)),
        ],
        compiler_params=pltpu.CompilerParams(
            collective_id=0, has_side_effects=True, vmem_limit_bytes=48 * 1024 * 1024
        ),
        cost_estimate=pl.CostEstimate(flops=2200000000, bytes_accessed=5000000, transcendentals=1048576),
    )(table, ocean_field, ocean_mask, kernels, gains, w_in, b_in, w_out, pick, place)


def solution(mesh):
    in_specs = (P("lat", "lon", None), P("lat", "lon"), P(), P(), P(), P(), P())
    out_specs = P("lat", "lon", None)
    body = functools.partial(local, mesh.shape["lat"], mesh.shape["lon"])
    return jax.shard_map(body, mesh=mesh, in_specs=in_specs, out_specs=out_specs, check_vma=False)
```

```python
import functools

import jax
import jax.numpy as jnp
import numpy as np
from jax import lax
from jax.experimental import pallas as pl
from jax.experimental.pallas import tpu as pltpu
from jax.sharding import PartitionSpec as P

MESH = pl.DeviceIdType.MESH
LEFT, RIGHT, UP, UP_LEFT, UP_RIGHT, DOWN, DOWN_LEFT, DOWN_RIGHT = range(8)


def row_tables(lat_count, tile_rows):
    total = lat_count * tile_rows
    rows = np.arange(-3, total + 3)
    cosine = np.cos(np.pi * ((rows + 0.5) / total - 0.5))
    cosine = np.where((rows >= 0) & (rows < total), cosine, 0.0)
    table = np.zeros((lat_count, 48), np.float32)
    for i in range(lat_count):
        near = cosine[i * tile_rows : i * tile_rows + tile_rows + 6]
        weight = sum(near[a : a + tile_rows] for a in range(7))
        table[i, : tile_rows + 6] = near
        table[i, 24 : 24 + tile_rows] = 7.0 / weight
    return table


def pick_matrix(tile):
    pick = np.zeros((2, 3 * tile, tile * tile), np.float32)
    for r in range(tile):
        for j in range(3):
            pick[0, 3 * r + j, r * tile + j] = 1.0
            pick[1, 3 * r + j, r * tile + tile - 3 + j] = 1.0
    return pick.reshape(6 * tile, tile * tile)


def place_matrix(tile):
    rows = tile + 6
    place = np.zeros((2, rows * 8, 3 * tile + 32), np.float32)
    for r in range(rows):
        for j in range(3):
            if r < 3:
                source = 7 + 3 * r + j
            elif r < 3 + tile:
                source = 16 + 3 * (r - 3) + j
            else:
                source = 16 + 3 * tile + 3 * (r - 3 - tile) + j
            place[0, r * 8 + 5 + j, source] = 1.0
            place[1, r * 8 + j, source] = 1.0
    return place


def kernel(
    lat_count, lon_count, layers,
    table_s, x_h, mask_h, taps_h, gains_h, w_in_h, b_in_h, w_out_h, pick_h, place_h,
    out_h,
    state, field, part, mask_i, mask_f, cos_v, inv_v, taps, spread, gains, w_in, b_in, w_out, pick, place,
    send_cols, recv_cols, recv_rows, load_sem, w_sem, send_sem, recv_sem,
):
    lat, lon = lax.axis_index("lat"), lax.axis_index("lon")
    left, right = lax.rem(lon + lon_count - 1, lon_count), lax.rem(lon + 1, lon_count)
    has_up, has_down = lat > 0, lat < lat_count - 1

    small = [
        pltpu.make_async_copy(src, dst, load_sem.at[i])
        for i, (src, dst) in enumerate(
            [
                (x_h, state.at[0]), (pick_h, pick), (mask_h, mask_i), (taps_h, taps),
                (place_h, place), (gains_h, gains), (b_in_h, b_in),
            ]
        )
    ]

    def weights(l):
        return (
            pltpu.make_async_copy(w_in_h.at[l], w_in.at[l], w_sem.at[0, l]),
            pltpu.make_async_copy(w_out_h.at[l], w_out.at[l], w_sem.at[1, l]),
        )

    for copy in small:
        copy.start()
    for l in range(layers):
        for copy in weights(l):
            copy.start()

    barrier = pltpu.get_barrier_semaphore()

    def greet(to_lat, to_lon):
        pl.semaphore_signal(barrier, inc=1, device_id=(to_lat, to_lon), device_id_type=MESH)

    greet(lat, left)
    greet(lat, right)

    @pl.when(has_up)
    def _():
        for other in (left, lon, right):
            greet(lat - 1, other)

    @pl.when(has_down)
    def _():
        for other in (left, lon, right):
            greet(lat + 1, other)

    @pl.when(jnp.logical_not(has_up))
    def _():
        recv_cols[:, :, 0:16] = jnp.zeros((layers, 2, 16, 256), jnp.bfloat16)
        recv_rows[:, 0] = jnp.zeros((layers, 3, 16, 256), jnp.bfloat16)

    @pl.when(jnp.logical_not(has_down))
    def _():
        recv_cols[:, :, 64:80] = jnp.zeros((layers, 2, 16, 256), jnp.bfloat16)
        recv_rows[:, 1] = jnp.zeros((layers, 3, 16, 256), jnp.bfloat16)

    for r in range(22):
        cos_v[r] = jnp.full((16, 128), table_s[lat, r], jnp.float32)
    for r in range(16):
        inv_v[r] = jnp.full((8, 128), table_s[lat, 24 + r], jnp.float32)

    small[2].wait()
    eye = lax.broadcasted_iota(jnp.int32, (16, 16), 0) == lax.broadcasted_iota(jnp.int32, (16, 16), 1)
    for r in range(16):
        cells = jnp.where(eye, mask_i[r : r + 1, :].astype(jnp.float32), 0.0)
        mask_f[r] = jnp.broadcast_to(jnp.sum(cells, axis=1, keepdims=True), (16, 128))
    small[0].wait()
    small[1].wait()

    def store_own(rows, cells, first):
        scale = cos_v[3 + first : 3 + first + rows]
        for half in range(2):
            field[half, 3 + first : 3 + first + rows, 8:24, :] = cells[:, :, half * 128 : half * 128 + 128] * scale

    store_own(16, state[0].astype(jnp.float32), 0)

    lats = 1
    for there in (has_up, has_down):
        lats = lats + there.astype(jnp.int32)
    pl.semaphore_wait(barrier, 3 * lats - 1)

    def copies(l):
        def remote(kind, src, dst, to_lat, to_lon):
            return pltpu.make_async_remote_copy(
                src_ref=src, dst_ref=dst, send_sem=send_sem.at[l, kind], recv_sem=recv_sem.at[l, kind],
                device_id=(to_lat, to_lon), device_id_type=MESH,
            )

        def side(kind, s, to_lon):
            return remote(kind, send_cols.at[l, s], recv_cols.at[l, 1 - s, 16:64], lat, to_lon)

        def corner(kind, s, src, dst, to_lat, to_lon):
            return remote(
                kind, send_cols.at[l, s, src : src + 16], recv_cols.at[l, 1 - s, dst : dst + 16], to_lat, to_lon
            )

        sides = [side(LEFT, 0, left), side(RIGHT, 1, right)]
        ups = [
            remote(UP, state.at[l, 0:3], recv_rows.at[l, 1], lat - 1, lon),
            corner(UP_LEFT, 0, 0, 64, lat - 1, left),
            corner(UP_RIGHT, 1, 0, 64, lat - 1, right),
        ]
        downs = [
            remote(DOWN, state.at[l, 13:16], recv_rows.at[l, 0], lat + 1, lon),
            corner(DOWN_LEFT, 0, 32, 0, lat + 1, left),
            corner(DOWN_RIGHT, 1, 32, 0, lat + 1, right),
        ]
        return sides, ups, downs

    def local_columns(g):
        return range(3, 7) if g == 0 else range(0, 4)

    def far_columns(g):
        return range(0, 3) if g == 0 else range(4, 7)

    def layer(l, carry):
        edges = jnp.dot(pick[...], state[l].reshape(256, 256), preferred_element_type=jnp.float32)
        edges = edges.astype(jnp.bfloat16)
        send_cols[l, 0] = edges[0:48]
        send_cols[l, 1] = edges[48:96]
        sides, ups, downs = copies(l)
        for copy in sides:
            copy.start()

        @pl.when(has_up)
        def _():
            for copy in ups:
                copy.start()

        @pl.when(has_down)
        def _():
            for copy in downs:
                copy.start()

        @pl.when(l == 0)
        def _():
            for copy in small[3:]:
                copy.wait()

            def spread_row(a, carry):
                for b in range(7):
                    row = taps[a, b]
                    for at in range(layers):
                        for half in range(2):
                            one = row[at : at + 1, half * 128 : half * 128 + 128]
                            spread[at, half, 7 * a + b] = jnp.broadcast_to(one, (8, 128))
                return carry

            lax.fori_loop(0, 7, spread_row, 0)

        def weight(half, a, b):
            return spread[l, half, 7 * a + b]

        def near(half, carry):
            for g in range(2):
                acc = jnp.zeros((16, 8, 128), jnp.float32)
                for b in local_columns(g):
                    start = 5 + 8 * g + b
                    x = field[half, 3:19, start : start + 8, :]
                    for a in range(7):
                        low, high = max(0, 3 - a), min(16, 19 - a)
                        add = acc[low:high] + weight(half, a, b) * x[low + a - 3 : high + a - 3]
                        pieces = [acc[:low]] * (low > 0) + [add] + [acc[high:]] * (high < 16)
                        acc = jnp.concatenate(pieces, axis=0) if len(pieces) > 1 else add
                part[half, :, 8 * g : 8 * g + 8, :] = acc
            return carry

        lax.fori_loop(0, 2, near, 0)

        for copy in sides:
            copy.wait_recv()

        @pl.when(has_down)
        def _():
            for copy in ups:
                copy.wait_recv()

        @pl.when(has_up)
        def _():
            for copy in downs:
                copy.wait_recv()

        for s in range(2):
            cells = recv_rows[l, s].astype(jnp.float32)
            scale = cos_v[19 * s : 19 * s + 3]
            columns = jnp.dot(place[s], recv_cols[l, s], preferred_element_type=jnp.float32).reshape(22, 8, 256)
            for half in range(2):
                lanes = slice(half * 128, half * 128 + 128)
                field[half, 19 * s : 19 * s + 3, 8:24, :] = cells[:, :, lanes] * scale
                field[half, :, 24 * s : 24 * s + 8, :] = columns[:, :, lanes] * cos_v[:, 0:8, :]

        def far(half, carry):
            for g in range(2):
                acc = part[half, :, 8 * g : 8 * g + 8, :]
                for b in far_columns(g):
                    start = 5 + 8 * g + b
                    x = field[half, :, start : start + 8, :]
                    for a in range(7):
                        acc = acc + weight(half, a, b) * x[a : a + 16]
                top, mid, low = acc[0:3], acc[3:13], acc[13:16]
                for b in local_columns(g):
                    start = 5 + 8 * g + b
                    above = field[half, 0:3, start : start + 8, :]
                    below = field[half, 19:22, start : start + 8, :]
                    for a in range(3):
                        add = top[0 : 3 - a] + weight(half, a, b) * above[a:3]
                        top = jnp.concatenate([add, top[3 - a :]], axis=0) if a > 0 else add
                    for a in range(4, 7):
                        add = low[6 - a :] + weight(half, a, b) * below[0 : a - 3]
                        low = jnp.concatenate([low[: 6 - a], add], axis=0) if a < 6 else add
                acc = jnp.concatenate([top, mid, low], axis=0) * inv_v[...]
                part[half, :, 8 * g : 8 * g + 8, :] = acc
            return carry

        lax.fori_loop(0, 2, far, 0)

        for copy in weights(l):
            copy.wait()
        gain = gains[pl.ds(l, 1), :]
        bias = b_in[pl.ds(l, 1), :]
        rows = 8
        for block in range(2):
            first = block * rows
            s0 = part[0, first : first + rows].reshape(rows * 16, 128)
            s1 = part[1, first : first + rows].reshape(rows * 16, 128)
            mean = jnp.sum(s0 * s0 + s1 * s1, axis=1, keepdims=True) * (1.0 / 256.0)
            scale = lax.rsqrt(mean + 1e-06)
            normed = jnp.concatenate([s0 * scale * gain[:, :128], s1 * scale * gain[:, 128:]], axis=1)
            half_v = 0.5 * (
                jnp.dot(normed.astype(jnp.bfloat16), w_in[l], preferred_element_type=jnp.float32) + bias
            )
            hidden = (half_v + half_v * jnp.tanh(half_v)).astype(jnp.bfloat16)
            update = jnp.dot(hidden, w_out[l], preferred_element_type=jnp.float32).reshape(rows, 16, 256)
            old = state[l, first : first + rows].astype(jnp.float32)
            wet = mask_f[first : first + rows]
            new = ((old + update) * jnp.concatenate([wet, wet], axis=2)).astype(jnp.bfloat16)
            state[l + 1, first : first + rows] = new
            store_own(rows, new.astype(jnp.float32), first)
        return carry

    lax.fori_loop(0, layers, layer, 0)

    final = pltpu.make_async_copy(state.at[layers], out_h, load_sem.at[7])
    final.start()

    def drain(l, carry):
        sides, ups, downs = copies(l)
        for copy in sides:
            copy.wait_send()

        @pl.when(has_up)
        def _():
            for copy in ups:
                copy.wait_send()

        @pl.when(has_down)
        def _():
            for copy in downs:
                copy.wait_send()

        return carry

    lax.fori_loop(0, layers, drain, 0)
    final.wait()


def local(lat_count, lon_count, ocean_field, ocean_mask, kernels, gains, w_in, b_in, w_out):
    layers = kernels.shape[0]
    bf16, f32 = jnp.bfloat16, jnp.float32
    table = jnp.asarray(row_tables(lat_count, ocean_field.shape[0]))
    pick = jnp.asarray(pick_matrix(16), bf16)
    place = jnp.asarray(place_matrix(16), bf16)
    taps = jnp.transpose(kernels, (1, 2, 0, 3))
    anywhere = pl.BlockSpec(memory_space=pltpu.HBM)
    return pl.pallas_call(
        functools.partial(kernel, lat_count, lon_count, layers),
        out_shape=jax.ShapeDtypeStruct(ocean_field.shape, bf16),
        in_specs=[pl.BlockSpec(memory_space=pltpu.SMEM)] + [anywhere] * 9,
        out_specs=anywhere,
        scratch_shapes=[
            pltpu.VMEM((layers + 1, 16, 16, 256), bf16),
            pltpu.VMEM((2, 22, 32, 128), f32),
            pltpu.VMEM((2, 16, 16, 128), f32),
            pltpu.VMEM((16, 16), jnp.int32),
            pltpu.VMEM((16, 16, 128), f32),
            pltpu.VMEM((22, 16, 128), f32),
            pltpu.VMEM((16, 8, 128), f32),
            pltpu.VMEM(taps.shape, f32),
            pltpu.VMEM((layers, 2, 49, 8, 128), f32),
            pltpu.VMEM(gains.shape, f32),
            pltpu.VMEM(w_in.shape, bf16),
            pltpu.VMEM(b_in.shape, f32),
            pltpu.VMEM(w_out.shape, bf16),
            pltpu.VMEM(pick.shape, bf16),
            pltpu.VMEM(place.shape, bf16),
            pltpu.VMEM((layers, 2, 48, 256), bf16),
            pltpu.VMEM((layers, 2, 80, 256), bf16),
            pltpu.VMEM((layers, 2, 3, 16, 256), bf16),
            pltpu.SemaphoreType.DMA((8,)),
            pltpu.SemaphoreType.DMA((2, layers)),
            pltpu.SemaphoreType.DMA((layers, 8)),
            pltpu.SemaphoreType.DMA((layers, 8)),
        ],
        compiler_params=pltpu.CompilerParams(
            collective_id=0, has_side_effects=True, vmem_limit_bytes=60 * 1024 * 1024
        ),
        cost_estimate=pl.CostEstimate(flops=2200000000, bytes_accessed=5000000, transcendentals=1048576),
    )(table, ocean_field, ocean_mask, taps, gains, w_in, b_in, w_out, pick, place)


def solution(mesh):
    in_specs = (P("lat", "lon", None), P("lat", "lon"), P(), P(), P(), P(), P())
    out_specs = P("lat", "lon", None)
    body = functools.partial(local, mesh.shape["lat"], mesh.shape["lon"])
    return jax.shard_map(body, mesh=mesh, in_specs=in_specs, out_specs=out_specs, check_vma=False)
```

```python
import functools

import jax
import jax.numpy as jnp
import numpy as np
from jax import lax
from jax.experimental import pallas as pl
from jax.experimental.pallas import tpu as pltpu
from jax.sharding import PartitionSpec as P

MESH = pl.DeviceIdType.MESH
LEFT, RIGHT, UP, UP_LEFT, UP_RIGHT, DOWN, DOWN_LEFT, DOWN_RIGHT = range(8)


def row_tables(lat_count, tile_rows):
    total = lat_count * tile_rows
    rows = np.arange(-6, total + 6)
    cosine = np.cos(np.pi * ((rows + 0.5) / total - 0.5))
    cosine = np.where((rows >= 0) & (rows < total), cosine, 0.0)
    table = np.zeros((lat_count, 64), np.float32)
    for i in range(lat_count):
        near = cosine[i * tile_rows : i * tile_rows + tile_rows + 12]
        weight = sum(near[a : a + tile_rows + 6] for a in range(7))
        table[i, : tile_rows + 12] = near
        table[i, 32 : 32 + tile_rows + 6] = 7.0 / weight
    return table


def pick_matrix(tile):
    pick = np.zeros((2, 6 * tile, tile * tile), np.float32)
    for r in range(tile):
        for j in range(6):
            pick[0, 6 * r + j, r * tile + j] = 1.0
            pick[1, 6 * r + j, r * tile + tile - 6 + j] = 1.0
    return pick.reshape(12 * tile, tile * tile)


def place_matrix(tile):
    rows = tile + 12
    place = np.zeros((2, rows * 8, 6 * tile + 96), np.float32)
    for r in range(rows):
        for j in range(6):
            if r < 6:
                source = 12 + 6 * r + j
            elif r < 6 + tile:
                source = 48 + 6 * (r - 6) + j
            else:
                source = 48 + 6 * tile + 6 * (r - 6 - tile) + j
            place[0, r * 8 + 2 + j, source] = 1.0
            place[1, r * 8 + j, source] = 1.0
    return place


def kernel(
    lat_count, lon_count, layers,
    table_s, x_h, mask_h, taps_h, gains_h, w_in_h, b_in_h, w_out_h, pick_h, place_h,
    out_h,
    state_0, state_1, final, field, plain, part, mask_i, wet, cos_v, inv_v, taps, spread, gains, w_in, b_in,
    w_out, pick, place,
    cols_out_0, cols_out_1, cols_in_0, cols_in_1, rows_in_0, rows_in_1, load_sem, w_sem, send_sem, recv_sem,
):
    lat, lon = lax.axis_index("lat"), lax.axis_index("lon")
    left, right = lax.rem(lon + lon_count - 1, lon_count), lax.rem(lon + 1, lon_count)
    has_up, has_down = lat > 0, lat < lat_count - 1
    state, cols_out = (state_0, state_1), (cols_out_0, cols_out_1)
    cols_in, rows_in = (cols_in_0, cols_in_1), (rows_in_0, rows_in_1)

    small = [
        pltpu.make_async_copy(src, dst, load_sem.at[i])
        for i, (src, dst) in enumerate(
            [
                (x_h, final), (pick_h, pick), (mask_h, mask_i), (taps_h, taps),
                (place_h, place), (gains_h, gains), (b_in_h, b_in),
            ]
        )
    ]

    def weights(l):
        return (
            pltpu.make_async_copy(w_in_h.at[l], w_in.at[l], w_sem.at[0, l]),
            pltpu.make_async_copy(w_out_h.at[l], w_out.at[l], w_sem.at[1, l]),
        )

    for copy in small:
        copy.start()
    for l in range(layers):
        for copy in weights(l):
            copy.start()

    barrier = pltpu.get_barrier_semaphore()

    def greet(to_lat, to_lon):
        pl.semaphore_signal(barrier, inc=1, device_id=(to_lat, to_lon), device_id_type=MESH)

    greet(lat, left)
    greet(lat, right)

    @pl.when(has_up)
    def _():
        for other in (left, lon, right):
            greet(lat - 1, other)

    @pl.when(has_down)
    def _():
        for other in (left, lon, right):
            greet(lat + 1, other)

    @pl.when(jnp.logical_not(has_up))
    def _():
        for p in range(2):
            width = cols_in[p].shape[2]
            cols_in[p][:, 0:48] = jnp.zeros((2, 48, width), jnp.bfloat16)
            rows_in[p][0] = jnp.zeros((6, 16, width), jnp.bfloat16)

    @pl.when(jnp.logical_not(has_down))
    def _():
        for p in range(2):
            width = cols_in[p].shape[2]
            cols_in[p][:, 144:192] = jnp.zeros((2, 48, width), jnp.bfloat16)
            rows_in[p][1] = jnp.zeros((6, 16, width), jnp.bfloat16)

    for r in range(28):
        cos_v[r] = jnp.full((8, 128), table_s[lat, r], jnp.float32)
    for r in range(22):
        inv_v[r] = jnp.full((8, 128), table_s[lat, 32 + r], jnp.float32)

    small[2].wait()
    eye = lax.broadcasted_iota(jnp.int32, (16, 16), 0) == lax.broadcasted_iota(jnp.int32, (16, 16), 1)
    for r in range(16):
        cells = jnp.where(eye, mask_i[r : r + 1, :].astype(jnp.float32), 0.0)
        cells = jnp.broadcast_to(jnp.sum(cells, axis=1, keepdims=True), (16, 128))
        wet[6 + r, 8:24, :] = cells
        state_0[r, :, 256:384] = cells.astype(jnp.bfloat16)
    small[0].wait()
    state_0[:, :, 0:256] = final[...]
    small[1].wait()

    def store(row, rows, column, columns, cells):
        scale = jnp.concatenate([cos_v[row : row + rows]] * (columns // 8), axis=1)
        for half in range(2):
            values = cells[:, :, half * 128 : half * 128 + 128]
            plain[half, row : row + rows, column : column + columns, :] = values
            field[half, row : row + rows, column : column + columns, :] = values * scale

    lats = 1
    for there in (has_up, has_down):
        lats = lats + there.astype(jnp.int32)
    pl.semaphore_wait(barrier, 3 * lats - 1)

    def copies(p):
        def remote(kind, src, dst, to_lat, to_lon):
            return pltpu.make_async_remote_copy(
                src_ref=src, dst_ref=dst, send_sem=send_sem.at[p, kind], recv_sem=recv_sem.at[p, kind],
                device_id=(to_lat, to_lon), device_id_type=MESH,
            )

        def side(kind, s, to_lon):
            return remote(kind, cols_out[p].at[s], cols_in[p].at[1 - s, 48:144], lat, to_lon)

        def corner(kind, s, src, dst, to_lat, to_lon):
            return remote(
                kind, cols_out[p].at[s, src : src + 48], cols_in[p].at[1 - s, dst : dst + 48], to_lat, to_lon
            )

        sides = [side(LEFT, 0, left), side(RIGHT, 1, right)]
        ups = [
            corner(UP_LEFT, 0, 0, 144, lat - 1, left),
            corner(UP_RIGHT, 1, 0, 144, lat - 1, right),
            remote(UP, state[p].at[0:6], rows_in[p].at[1], lat - 1, lon),
        ]
        downs = [
            corner(DOWN_LEFT, 0, 48, 0, lat + 1, left),
            corner(DOWN_RIGHT, 1, 48, 0, lat + 1, right),
            remote(DOWN, state[p].at[10:16], rows_in[p].at[0], lat + 1, lon),
        ]
        return sides, ups, downs

    def taps_over(l, half, acc, start, first, rows):
        for b in range(7):
            x = field[half, first : first + rows + 6, start - 3 + b : start + 5 + b, :]
            for a in range(7):
                acc = acc + spread[l, half, 7 * a + b] * x[a : a + rows]
        return acc

    def mix(l, rows, first_row, column, columns, block_rows, emit):
        for copy in weights(l):
            copy.wait()
        gain, bias = gains[l : l + 1, :], b_in[l : l + 1, :]
        for first in range(0, rows, block_rows):
            cells = block_rows * columns
            s0 = part[0, first : first + block_rows, 0:columns].reshape(cells, 128)
            s1 = part[1, first : first + block_rows, 0:columns].reshape(cells, 128)
            mean = jnp.sum(s0 * s0 + s1 * s1, axis=1, keepdims=True) * (1.0 / 256.0)
            scale = lax.rsqrt(mean + 1e-06)
            normed = jnp.concatenate([s0 * scale * gain[:, :128], s1 * scale * gain[:, 128:]], axis=1)
            half_v = 0.5 * (
                jnp.dot(normed.astype(jnp.bfloat16), w_in[l], preferred_element_type=jnp.float32) + bias
            )
            hidden = (half_v + half_v * jnp.tanh(half_v)).astype(jnp.bfloat16)
            update = jnp.dot(hidden, w_out[l], preferred_element_type=jnp.float32)
            update = update.reshape(block_rows, columns, 256)
            row = first_row + first
            here = (slice(row, row + block_rows), slice(column, column + columns))
            old = jnp.concatenate([plain[(0, *here)], plain[(1, *here)]], axis=2)
            dry = wet[here]
            new = (old + update) * jnp.concatenate([dry, dry], axis=2)
            emit(row, new.astype(jnp.bfloat16))

    for p in range(2):
        l = 2 * p
        edges = jnp.dot(
            pick[...], state[p][...].reshape(256, state[p].shape[2]), preferred_element_type=jnp.float32
        ).astype(jnp.bfloat16)
        cols_out[p][0] = edges[0:96]
        cols_out[p][1] = edges[96:192]
        sides, ups, downs = copies(p)

        @pl.when(has_up)
        def _(ups=ups):
            for copy in ups:
                copy.start()

        @pl.when(has_down)
        def _(downs=downs):
            for copy in downs:
                copy.start()

        for copy in sides:
            copy.start()

        if p == 0:
            store(6, 16, 8, 16, state[0][:, :, 0:256].astype(jnp.float32))
            for copy in small[3:]:
                copy.wait()

            def spread_row(a, carry):
                for b in range(7):
                    row = taps[a, b]
                    for at in range(layers):
                        for half in range(2):
                            one = row[at : at + 1, half * 128 : half * 128 + 128]
                            spread[at, half, 7 * a + b] = jnp.broadcast_to(one, (8, 128))
                return carry

            lax.fori_loop(0, 7, spread_row, 0)

        def near(half, carry, l=l):
            acc = jnp.zeros((22, 8, 128), jnp.float32)
            for b in range(7):
                x = field[half, 6:22, 10 + b : 18 + b, :]
                for a in range(7):
                    low, high = max(0, 6 - a), 22 - a
                    add = acc[low:high] + spread[l, half, 7 * a + b] * x[low + a - 6 : high + a - 6]
                    pieces = [acc[:low]] * (low > 0) + [add] + [acc[high:]] * (high < 22)
                    acc = jnp.concatenate(pieces, axis=0)
            part[half, :, 8:16, :] = acc
            return carry

        lax.fori_loop(0, 2, near, 0)

        for copy in sides:
            copy.wait_recv()

        @pl.when(has_down)
        def _(ups=ups):
            for copy in ups:
                copy.wait_recv()

        @pl.when(has_up)
        def _(downs=downs):
            for copy in downs:
                copy.wait_recv()

        for s in range(2):
            cells = rows_in[p][s].astype(jnp.float32)
            columns = jnp.dot(place[s], cols_in[p][s], preferred_element_type=jnp.float32)
            columns = columns.reshape(28, 8, cols_in[p].shape[2])
            store(22 * s, 6, 8, 16, cells[:, :, 0:256])
            store(0, 28, 24 * s, 8, columns[:, :, 0:256])
            if p == 0:
                wet[22 * s : 22 * s + 6, 8:24, :] = cells[:, :, 256:384]
                wet[:, 24 * s : 24 * s + 8, :] = columns[:, :, 256:384]

        def far(half, carry, l=l):
            acc = part[half, :, 8:16, :]
            top, mid, low = acc[0:6], acc[6:16], acc[16:22]
            for b in range(7):
                above = field[half, 0:6, 10 + b : 18 + b, :]
                below = field[half, 22:28, 10 + b : 18 + b, :]
                for a in range(6):
                    add = top[0 : 6 - a] + spread[l, half, 7 * a + b] * above[a:6]
                    top = jnp.concatenate([add, top[6 - a :]], axis=0) if a > 0 else add
                for a in range(1, 7):
                    add = low[6 - a :] + spread[l, half, 7 * a + b] * below[0:a]
                    low = jnp.concatenate([low[: 6 - a], add], axis=0) if a < 6 else add
            part[half, :, 8:16, :] = jnp.concatenate([top, mid, low], axis=0) * inv_v[...]
            for g in (0, 2):
                acc = taps_over(l, half, jnp.zeros((22, 8, 128), jnp.float32), 5 + 8 * g, 0, 22)
                part[half, :, 8 * g : 8 * g + 8, :] = acc * inv_v[...]
            return carry

        lax.fori_loop(0, 2, far, 0)

        def emit_wide(row, new):
            store(row, new.shape[0], 5, 24, new.astype(jnp.float32))

        mix(l, 22, 3, 5, 24, 11, emit_wide)

        def own(half, carry, l=l):
            for g in range(2):
                acc = taps_over(l + 1, half, jnp.zeros((16, 8, 128), jnp.float32), 8 + 8 * g, 3, 16)
                part[half, 0:16, 8 * g : 8 * g + 8, :] = acc * inv_v[3:19]
            return carry

        lax.fori_loop(0, 2, own, 0)

        def emit_own(row, new, p=p):
            if p == 0:
                state_1[row - 6 : row - 6 + new.shape[0]] = new
                store(row, new.shape[0], 8, 16, new.astype(jnp.float32))
            else:
                final[row - 6 : row - 6 + new.shape[0]] = new

        mix(l + 1, 16, 6, 8, 16, 8, emit_own)

    result = pltpu.make_async_copy(final, out_h, load_sem.at[7])
    result.start()

    for p in range(2):
        sides, ups, downs = copies(p)
        for copy in sides:
            copy.wait_send()

        @pl.when(has_up)
        def _(ups=ups):
            for copy in ups:
                copy.wait_send()

        @pl.when(has_down)
        def _(downs=downs):
            for copy in downs:
                copy.wait_send()

    result.wait()


def local(lat_count, lon_count, ocean_field, ocean_mask, kernels, gains, w_in, b_in, w_out):
    layers = kernels.shape[0]
    bf16, f32 = jnp.bfloat16, jnp.float32
    table = jnp.asarray(row_tables(lat_count, ocean_field.shape[0]))
    pick = jnp.asarray(pick_matrix(16), bf16)
    place = jnp.asarray(place_matrix(16), bf16)
    taps = jnp.transpose(kernels, (1, 2, 0, 3))
    anywhere = pl.BlockSpec(memory_space=pltpu.HBM)
    return pl.pallas_call(
        functools.partial(kernel, lat_count, lon_count, layers),
        out_shape=jax.ShapeDtypeStruct(ocean_field.shape, bf16),
        in_specs=[pl.BlockSpec(memory_space=pltpu.SMEM)] + [anywhere] * 9,
        out_specs=anywhere,
        scratch_shapes=[
            pltpu.VMEM((16, 16, 384), bf16),
            pltpu.VMEM((16, 16, 256), bf16),
            pltpu.VMEM((16, 16, 256), bf16),
            pltpu.VMEM((2, 28, 32, 128), f32),
            pltpu.VMEM((2, 28, 32, 128), f32),
            pltpu.VMEM((2, 22, 24, 128), f32),
            pltpu.VMEM((16, 16), jnp.int32),
            pltpu.VMEM((28, 32, 128), f32),
            pltpu.VMEM((28, 8, 128), f32),
            pltpu.VMEM((22, 8, 128), f32),
            pltpu.VMEM(taps.shape, f32),
            pltpu.VMEM((layers, 2, 49, 8, 128), f32),
            pltpu.VMEM(gains.shape, f32),
            pltpu.VMEM(w_in.shape, bf16),
            pltpu.VMEM(b_in.shape, f32),
            pltpu.VMEM(w_out.shape, bf16),
            pltpu.VMEM(pick.shape, bf16),
            pltpu.VMEM(place.shape, bf16),
            pltpu.VMEM((2, 96, 384), bf16),
            pltpu.VMEM((2, 96, 256), bf16),
            pltpu.VMEM((2, 192, 384), bf16),
            pltpu.VMEM((2, 192, 256), bf16),
            pltpu.VMEM((2, 6, 16, 384), bf16),
            pltpu.VMEM((2, 6, 16, 256), bf16),
            pltpu.SemaphoreType.DMA((8,)),
            pltpu.SemaphoreType.DMA((2, layers)),
            pltpu.SemaphoreType.DMA((2, 8)),
            pltpu.SemaphoreType.DMA((2, 8)),
        ],
        compiler_params=pltpu.CompilerParams(
            collective_id=0, has_side_effects=True, vmem_limit_bytes=60 * 1024 * 1024
        ),
        cost_estimate=pl.CostEstimate(flops=2200000000, bytes_accessed=5000000, transcendentals=1048576),
    )(table, ocean_field, ocean_mask, taps, gains, w_in, b_in, w_out, pick, place)


def solution(mesh):
    in_specs = (P("lat", "lon", None), P("lat", "lon"), P(), P(), P(), P(), P())
    out_specs = P("lat", "lon", None)
    body = functools.partial(local, mesh.shape["lat"], mesh.shape["lon"])
    return jax.shard_map(body, mesh=mesh, in_specs=in_specs, out_specs=out_specs, check_vma=False)
```

```python
import functools

import jax
import jax.numpy as jnp
import numpy as np
from jax import lax
from jax.experimental import pallas as pl
from jax.experimental.pallas import tpu as pltpu
from jax.sharding import PartitionSpec as P

MESH = pl.DeviceIdType.MESH
LEFT, RIGHT, UP, UP_LEFT, UP_RIGHT, DOWN, DOWN_LEFT, DOWN_RIGHT = range(8)


def row_tables(lat_count, tile_rows):
    total = lat_count * tile_rows
    rows = np.arange(-6, total + 6)
    cosine = np.cos(np.pi * ((rows + 0.5) / total - 0.5))
    cosine = np.where((rows >= 0) & (rows < total), cosine, 0.0)
    table = np.zeros((lat_count, 64), np.float32)
    for i in range(lat_count):
        near = cosine[i * tile_rows : i * tile_rows + tile_rows + 12]
        weight = sum(near[a : a + tile_rows + 6] for a in range(7))
        table[i, : tile_rows + 12] = near
        table[i, 32 : 32 + tile_rows + 6] = 7.0 / weight
    return table


def pick_matrix(tile):
    pick = np.zeros((2, 6 * tile, tile * tile), np.float32)
    for r in range(tile):
        for j in range(6):
            pick[0, 6 * r + j, r * tile + j] = 1.0
            pick[1, 6 * r + j, r * tile + tile - 6 + j] = 1.0
    return pick.reshape(12 * tile, tile * tile)


def place_matrix(tile):
    rows = tile + 12
    place = np.zeros((2, rows * 8, 6 * tile + 96), np.float32)
    for r in range(rows):
        for j in range(6):
            if r < 6:
                source = 12 + 6 * r + j
            elif r < 6 + tile:
                source = 48 + 6 * (r - 6) + j
            else:
                source = 48 + 6 * tile + 6 * (r - 6 - tile) + j
            place[0, r * 8 + 2 + j, source] = 1.0
            place[1, r * 8 + j, source] = 1.0
    return place


def kernel(
    lat_count, lon_count, layers,
    table_s, x_h, mask_h, taps_h, gains_h, w_in_h, b_in_h, w_out_h, pick_h, place_h,
    out_h,
    state_0, state_1, final, field, plain, part, mask_i, wet, cos_v, inv_v, taps, spread, gains, w_in, b_in,
    w_out, pick, place,
    cols_out_0, cols_out_1, cols_in_0, cols_in_1, rows_in_0, rows_in_1, load_sem, w_sem, send_sem, recv_sem,
):
    lat, lon = lax.axis_index("lat"), lax.axis_index("lon")
    left, right = lax.rem(lon + lon_count - 1, lon_count), lax.rem(lon + 1, lon_count)
    has_up, has_down = lat > 0, lat < lat_count - 1
    state, cols_out = (state_0, state_1), (cols_out_0, cols_out_1)
    cols_in, rows_in = (cols_in_0, cols_in_1), (rows_in_0, rows_in_1)

    small = [
        pltpu.make_async_copy(src, dst, load_sem.at[i])
        for i, (src, dst) in enumerate(
            [
                (x_h, final), (pick_h, pick), (mask_h, mask_i), (taps_h, taps),
                (place_h, place), (gains_h, gains), (b_in_h, b_in),
            ]
        )
    ]

    def weights(l):
        return (
            pltpu.make_async_copy(w_in_h.at[l], w_in.at[l], w_sem.at[0, l]),
            pltpu.make_async_copy(w_out_h.at[l], w_out.at[l], w_sem.at[1, l]),
        )

    for copy in small:
        copy.start()
    for l in range(layers):
        for copy in weights(l):
            copy.start()

    barrier = pltpu.get_barrier_semaphore()

    def greet(to_lat, to_lon):
        pl.semaphore_signal(barrier, inc=1, device_id=(to_lat, to_lon), device_id_type=MESH)

    greet(lat, left)
    greet(lat, right)

    @pl.when(has_up)
    def _():
        for other in (left, lon, right):
            greet(lat - 1, other)

    @pl.when(has_down)
    def _():
        for other in (left, lon, right):
            greet(lat + 1, other)

    @pl.when(jnp.logical_not(has_up))
    def _():
        for p in range(2):
            width = cols_in[p].shape[2]
            cols_in[p][:, 0:48] = jnp.zeros((2, 48, width), jnp.bfloat16)
            rows_in[p][0] = jnp.zeros((6, 16, width), jnp.bfloat16)

    @pl.when(jnp.logical_not(has_down))
    def _():
        for p in range(2):
            width = cols_in[p].shape[2]
            cols_in[p][:, 144:192] = jnp.zeros((2, 48, width), jnp.bfloat16)
            rows_in[p][1] = jnp.zeros((6, 16, width), jnp.bfloat16)

    for r in range(28):
        cos_v[r] = jnp.full((8, 128), table_s[lat, r], jnp.float32)
    for r in range(22):
        inv_v[r] = jnp.full((8, 128), table_s[lat, 32 + r], jnp.float32)

    small[2].wait()
    eye = lax.broadcasted_iota(jnp.int32, (16, 16), 0) == lax.broadcasted_iota(jnp.int32, (16, 16), 1)
    for r in range(16):
        cells = jnp.where(eye, mask_i[r : r + 1, :].astype(jnp.float32), 0.0)
        cells = jnp.broadcast_to(jnp.sum(cells, axis=1, keepdims=True), (16, 128))
        wet[6 + r, 8:24, :] = cells
        state_0[r, :, 256:384] = cells.astype(jnp.bfloat16)
    small[0].wait()
    state_0[:, :, 0:256] = final[...]
    small[1].wait()

    def store(row, rows, column, columns, cells):
        scale = jnp.concatenate([cos_v[row : row + rows]] * (columns // 8), axis=1)
        for half in range(2):
            values = cells[:, :, half * 128 : half * 128 + 128]
            plain[half, row : row + rows, column : column + columns, :] = values
            field[half, row : row + rows, column : column + columns, :] = values * scale

    lats = 1
    for there in (has_up, has_down):
        lats = lats + there.astype(jnp.int32)
    pl.semaphore_wait(barrier, 3 * lats - 1)

    def copies(p):
        def remote(kind, src, dst, to_lat, to_lon):
            return pltpu.make_async_remote_copy(
                src_ref=src, dst_ref=dst, send_sem=send_sem.at[p, kind], recv_sem=recv_sem.at[p, kind],
                device_id=(to_lat, to_lon), device_id_type=MESH,
            )

        def side(kind, s, to_lon):
            return remote(kind, cols_out[p].at[s], cols_in[p].at[1 - s, 48:144], lat, to_lon)

        def corner(kind, s, src, dst, to_lat, to_lon):
            return remote(
                kind, cols_out[p].at[s, src : src + 48], cols_in[p].at[1 - s, dst : dst + 48], to_lat, to_lon
            )

        sides = [side(LEFT, 0, left), side(RIGHT, 1, right)]
        ups = [
            corner(UP_LEFT, 0, 0, 144, lat - 1, left),
            corner(UP_RIGHT, 1, 0, 144, lat - 1, right),
            remote(UP, state[p].at[0:6], rows_in[p].at[1], lat - 1, lon),
        ]
        downs = [
            corner(DOWN_LEFT, 0, 48, 0, lat + 1, left),
            corner(DOWN_RIGHT, 1, 48, 0, lat + 1, right),
            remote(DOWN, state[p].at[10:16], rows_in[p].at[0], lat + 1, lon),
        ]
        return sides, ups, downs

    def taps_over(l, half, acc, start, first, rows):
        for b in range(7):
            x = field[half, first : first + rows + 6, start - 3 + b : start + 5 + b, :]
            for a in range(7):
                acc = acc + spread[l, half, 7 * a + b] * x[a : a + rows]
        return acc

    def mix(l, rows, first_row, column, columns, block_rows, emit):
        for copy in weights(l):
            copy.wait()
        gain, bias = gains[l : l + 1, :], b_in[l : l + 1, :]
        for first in range(0, rows, block_rows):
            cells = block_rows * columns
            s0 = part[0, first : first + block_rows, 0:columns].reshape(cells, 128)
            s1 = part[1, first : first + block_rows, 0:columns].reshape(cells, 128)
            mean = jnp.sum(s0 * s0 + s1 * s1, axis=1, keepdims=True) * (1.0 / 256.0)
            scale = lax.rsqrt(mean + 1e-06)
            normed = jnp.concatenate([s0 * scale * gain[:, :128], s1 * scale * gain[:, 128:]], axis=1)
            half_v = 0.5 * (
                jnp.dot(normed.astype(jnp.bfloat16), w_in[l], preferred_element_type=jnp.float32) + bias
            )
            hidden = (half_v + half_v * jnp.tanh(half_v)).astype(jnp.bfloat16)
            update = jnp.dot(hidden, w_out[l], preferred_element_type=jnp.float32)
            update = update.reshape(block_rows, columns, 256)
            row = first_row + first
            here = (slice(row, row + block_rows), slice(column, column + columns))
            old = jnp.concatenate([plain[(0, *here)], plain[(1, *here)]], axis=2)
            dry = wet[here]
            new = (old + update) * jnp.concatenate([dry, dry], axis=2)
            emit(row, new.astype(jnp.bfloat16))

    for p in range(2):
        l = 2 * p
        sides, ups, downs = copies(p)

        @pl.when(has_up)
        def _(ups=ups):
            ups[2].start()

        @pl.when(has_down)
        def _(downs=downs):
            downs[2].start()

        edges = jnp.dot(
            pick[...], state[p][...].reshape(256, state[p].shape[2]), preferred_element_type=jnp.float32
        ).astype(jnp.bfloat16)
        cols_out[p][0] = edges[0:96]
        cols_out[p][1] = edges[96:192]

        @pl.when(has_up)
        def _(ups=ups):
            for copy in ups[:2]:
                copy.start()

        @pl.when(has_down)
        def _(downs=downs):
            for copy in downs[:2]:
                copy.start()

        for copy in sides:
            copy.start()

        store(6, 16, 8, 16, state[p][:, :, 0:256].astype(jnp.float32))
        if p == 0:
            for copy in small[3:]:
                copy.wait()

            def spread_row(a, carry):
                for b in range(7):
                    row = taps[a, b]
                    for at in range(layers):
                        for half in range(2):
                            one = row[at : at + 1, half * 128 : half * 128 + 128]
                            spread[at, half, 7 * a + b] = jnp.broadcast_to(one, (8, 128))
                return carry

            lax.fori_loop(0, 7, spread_row, 0)

        def near(half, carry, l=l):
            acc = jnp.zeros((22, 8, 128), jnp.float32)
            for b in range(7):
                x = field[half, 6:22, 10 + b : 18 + b, :]
                for a in range(7):
                    low, high = max(0, 6 - a), 22 - a
                    add = acc[low:high] + spread[l, half, 7 * a + b] * x[low + a - 6 : high + a - 6]
                    pieces = [acc[:low]] * (low > 0) + [add] + [acc[high:]] * (high < 22)
                    acc = jnp.concatenate(pieces, axis=0)
            part[half, :, 8:16, :] = acc
            return carry

        lax.fori_loop(0, 2, near, 0)

        for copy in sides:
            copy.wait_recv()

        @pl.when(has_down)
        def _(ups=ups):
            for copy in ups:
                copy.wait_recv()

        @pl.when(has_up)
        def _(downs=downs):
            for copy in downs:
                copy.wait_recv()

        for s in range(2):
            cells = rows_in[p][s].astype(jnp.float32)
            columns = jnp.dot(place[s], cols_in[p][s], preferred_element_type=jnp.float32)
            columns = columns.reshape(28, 8, cols_in[p].shape[2])
            store(22 * s, 6, 8, 16, cells[:, :, 0:256])
            store(0, 28, 24 * s, 8, columns[:, :, 0:256])
            if p == 0:
                wet[22 * s : 22 * s + 6, 8:24, :] = cells[:, :, 256:384]
                wet[:, 24 * s : 24 * s + 8, :] = columns[:, :, 256:384]

        def far(half, carry, l=l):
            acc = part[half, :, 8:16, :]
            top, mid, low = acc[0:6], acc[6:16], acc[16:22]
            for b in range(7):
                above = field[half, 0:6, 10 + b : 18 + b, :]
                below = field[half, 22:28, 10 + b : 18 + b, :]
                for a in range(6):
                    add = top[0 : 6 - a] + spread[l, half, 7 * a + b] * above[a:6]
                    top = jnp.concatenate([add, top[6 - a :]], axis=0) if a > 0 else add
                for a in range(1, 7):
                    add = low[6 - a :] + spread[l, half, 7 * a + b] * below[0:a]
                    low = jnp.concatenate([low[: 6 - a], add], axis=0) if a < 6 else add
            part[half, :, 8:16, :] = jnp.concatenate([top, mid, low], axis=0) * inv_v[...]
            for g in (0, 2):
                acc = taps_over(l, half, jnp.zeros((22, 8, 128), jnp.float32), 5 + 8 * g, 0, 22)
                part[half, :, 8 * g : 8 * g + 8, :] = acc * inv_v[...]
            return carry

        lax.fori_loop(0, 2, far, 0)

        def emit_wide(row, new):
            store(row, new.shape[0], 5, 24, new.astype(jnp.float32))

        mix(l, 22, 3, 5, 24, 22, emit_wide)

        def own(half, carry, l=l):
            for g in range(2):
                acc = taps_over(l + 1, half, jnp.zeros((16, 8, 128), jnp.float32), 8 + 8 * g, 3, 16)
                part[half, 0:16, 8 * g : 8 * g + 8, :] = acc * inv_v[3:19]
            return carry

        lax.fori_loop(0, 2, own, 0)

        def emit_own(row, new, p=p):
            if p == 0:
                state_1[row - 6 : row - 6 + new.shape[0]] = new
            else:
                final[row - 6 : row - 6 + new.shape[0]] = new

        mix(l + 1, 16, 6, 8, 16, 16, emit_own)

    result = pltpu.make_async_copy(final, out_h, load_sem.at[7])
    result.start()

    for p in range(2):
        sides, ups, downs = copies(p)
        for copy in sides:
            copy.wait_send()

        @pl.when(has_up)
        def _(ups=ups):
            for copy in ups:
                copy.wait_send()

        @pl.when(has_down)
        def _(downs=downs):
            for copy in downs:
                copy.wait_send()

    result.wait()


def local(lat_count, lon_count, ocean_field, ocean_mask, kernels, gains, w_in, b_in, w_out):
    layers = kernels.shape[0]
    bf16, f32 = jnp.bfloat16, jnp.float32
    table = jnp.asarray(row_tables(lat_count, ocean_field.shape[0]))
    pick = jnp.asarray(pick_matrix(16), bf16)
    place = jnp.asarray(place_matrix(16), bf16)
    taps = jnp.transpose(kernels, (1, 2, 0, 3))
    anywhere = pl.BlockSpec(memory_space=pltpu.HBM)
    return pl.pallas_call(
        functools.partial(kernel, lat_count, lon_count, layers),
        out_shape=jax.ShapeDtypeStruct(ocean_field.shape, bf16),
        in_specs=[pl.BlockSpec(memory_space=pltpu.SMEM)] + [anywhere] * 9,
        out_specs=anywhere,
        scratch_shapes=[
            pltpu.VMEM((16, 16, 384), bf16),
            pltpu.VMEM((16, 16, 256), bf16),
            pltpu.VMEM((16, 16, 256), bf16),
            pltpu.VMEM((2, 28, 32, 128), f32),
            pltpu.VMEM((2, 28, 32, 128), f32),
            pltpu.VMEM((2, 22, 24, 128), f32),
            pltpu.VMEM((16, 16), jnp.int32),
            pltpu.VMEM((28, 32, 128), f32),
            pltpu.VMEM((28, 8, 128), f32),
            pltpu.VMEM((22, 8, 128), f32),
            pltpu.VMEM(taps.shape, f32),
            pltpu.VMEM((layers, 2, 49, 8, 128), f32),
            pltpu.VMEM(gains.shape, f32),
            pltpu.VMEM(w_in.shape, bf16),
            pltpu.VMEM(b_in.shape, f32),
            pltpu.VMEM(w_out.shape, bf16),
            pltpu.VMEM(pick.shape, bf16),
            pltpu.VMEM(place.shape, bf16),
            pltpu.VMEM((2, 96, 384), bf16),
            pltpu.VMEM((2, 96, 256), bf16),
            pltpu.VMEM((2, 192, 384), bf16),
            pltpu.VMEM((2, 192, 256), bf16),
            pltpu.VMEM((2, 6, 16, 384), bf16),
            pltpu.VMEM((2, 6, 16, 256), bf16),
            pltpu.SemaphoreType.DMA((8,)),
            pltpu.SemaphoreType.DMA((2, layers)),
            pltpu.SemaphoreType.DMA((2, 8)),
            pltpu.SemaphoreType.DMA((2, 8)),
        ],
        compiler_params=pltpu.CompilerParams(
            collective_id=0, has_side_effects=True, vmem_limit_bytes=60 * 1024 * 1024
        ),
        cost_estimate=pl.CostEstimate(flops=2200000000, bytes_accessed=5000000, transcendentals=1048576),
    )(table, ocean_field, ocean_mask, taps, gains, w_in, b_in, w_out, pick, place)


def solution(mesh):
    in_specs = (P("lat", "lon", None), P("lat", "lon"), P(), P(), P(), P(), P())
    out_specs = P("lat", "lon", None)
    body = functools.partial(local, mesh.shape["lat"], mesh.shape["lon"])
    return jax.shard_map(body, mesh=mesh, in_specs=in_specs, out_specs=out_specs, check_vma=False)
```
